512 devices in a mesh: wide: 32 (over z, y_hi), narrow: 16 (over y_lo, x, core).
Axes of the slice: x: 4, y: 8 (y_hi: 4, y_lo: 2; y = y_hi * 2 + y_lo), z: 8, core: 2. Of those that a mesh axis runs over, the one named last changes fastest.
Arguments:
- images: bfloat16 [131072, 1152], P(('wide', 'narrow')), may hold values from -0.1875 to 0.1875
- texts: bfloat16 [131072, 1152], P(('wide', 'narrow')), may hold values from -0.1875 to 0.1875
- labels: int32 [131072], P(('wide', 'narrow')), may hold values from 0 to 131071, as said below
- log_scale: float32 [1], replicated, may hold values from 1 to 2.3
- bias: float32 [1], replicated, may hold values from -4 to -2
Outputs:
- grad_images: float32 [131072, 1152], P(('wide', 'narrow'))
- grad_texts: float32 [131072, 1152], P(('wide', 'narrow'))
The draws below stay inside these ranges and needn't reach their ends.
Inputs may be any that keep to these rules, and one draw needn't show every extreme that they name: labels_i names a text row of the same block of 256 rows as row i, and the labels of each block are a permutation of that block's rows.
All inputs are finite; a program needn't handle non-finite values.
Results may differ from the reference program's by a relative error of at most 0.0042.
Values may be sent and summed in bfloat16 or wider, within the bound.
No kernel may reach another device: no remote copies, remote signals or barrier semaphores. Data moves between devices by JAX's collectives and lax.ppermute only.
A program may use at most 64 MiB of HBM per device.

```python
import jax
import jax.numpy as jnp
from jax import lax

D = 1152
BLOCK = 256
WINDOW = 4
BATCH = 131072
N_WIDE = 32
N_NARROW = 16


def draw_labels(key, part):
    key = jax.random.fold_in(key, 7)
    blocks = BATCH // BLOCK
    subkeys = jax.random.split(key, blocks)
    orders = jax.vmap(lambda single: jax.random.permutation(single, BLOCK))(subkeys)
    starts = jnp.arange(blocks, dtype=jnp.int32)[:, None] * BLOCK
    return (orders.astype(jnp.int32) + starts).reshape(BATCH)


def level_of(stream_key, shape, cuts, smallest, top_value):
    def one(dim, blocks):
        heights = jax.random.uniform(jax.random.fold_in(jax.random.fold_in(stream_key, 6), dim), (blocks,), jnp.float32, smallest / len(cuts), top_value / len(cuts))
        return jnp.repeat(jnp.exp(heights), shape[dim] // blocks).reshape((-1,) + (1,) * (len(shape) - dim - 1))

    factor_of = one(*cuts[0])
    for cut in cuts[1:]:
        factor_of = factor_of * one(*cut)
    return factor_of


def noise(stream_key, extent, spread, bound, shards=(), held_as=jnp.bfloat16):
    result = jax.random.normal(stream_key, extent, jnp.float32) * spread
    if len(shards) > 0:
        result = level_of(stream_key, extent, shards, -0.22, 0.18) * result
    return jnp.clip(result, min=-bound, max=bound).astype(held_as)


def setup_inputs(seed: int = 0) -> dict:
    keys = jax.random.split(jax.random.key(seed), 6)
    images = noise(keys[0], (BATCH, D), D ** -0.5, 0.1875, ((0, 512),))
    texts = noise(keys[1], (BATCH, D), D ** -0.5, 0.1875, ((0, 512),))
    labels = draw_labels(jax.random.fold_in(keys[5], 71), 0)
    log_scale = jnp.clip(jax.random.uniform(keys[3], (1,), jnp.float32, 1.0, 2.3), 1.0, 2.3)
    bias = jnp.clip(jax.random.uniform(keys[4], (1,), jnp.float32, -4.0, -2.0), -4.0, -2.0)
    return {"images": images, "texts": texts, "labels": labels, "log_scale": log_scale, "bias": bias}


EPS = 1e-06

def normalize(vectors):
    floats = vectors.astype(jnp.float32)
    inverse = lax.rsqrt(lax.optimization_barrier(jnp.sum(floats * floats, axis=-1, keepdims=True)) + EPS)
    return (floats * inverse, inverse)

def unit_backward(unit_rows, inverse, upstream):
    return inverse * (upstream - unit_rows * lax.optimization_barrier(jnp.sum(unit_rows * upstream, axis=-1, keepdims=True)))

def reference(images, texts, labels, log_scale, bias):
    grid_shape = (N_WIDE, N_NARROW, BLOCK, D)
    image_unit, image_inverse = normalize(images)
    text_unit, text_inverse = normalize(texts)
    image_half = lax.optimization_barrier(image_unit.astype(jnp.bfloat16)).astype(jnp.float32).reshape(grid_shape)
    text_half = lax.optimization_barrier(text_unit.astype(jnp.bfloat16)).astype(jnp.float32).reshape(grid_shape)
    temper = jnp.exp(log_scale[0])
    offset = bias[0]
    label_grid = labels.reshape(N_WIDE, N_NARROW, BLOCK, 1)
    index_grid = jnp.arange(BATCH, dtype=jnp.int32).reshape(N_WIDE, N_NARROW, 1, BLOCK)
    image_grad = jnp.zeros(grid_shape, jnp.float32)
    text_grad = jnp.zeros(grid_shape, jnp.float32)
    for wide_step in range(2):
        for narrow_step in range(WINDOW):
            offsets = (wide_step, narrow_step + wide_step * (WINDOW - 1))
            visitor = jnp.roll(text_half, offsets, axis=(0, 1))
            target = jnp.roll(index_grid, offsets, axis=(0, 1))
            scores = jnp.einsum('wnid,wnjd->wnij', image_half, visitor)
            logits = temper * scores + offset
            positive = (label_grid == target).astype(jnp.float32)
            residual = jax.nn.sigmoid(logits) - positive
            weighted = lax.optimization_barrier((temper * residual).astype(jnp.bfloat16)).astype(jnp.float32)
            image_grad = image_grad + jnp.einsum('wnij,wnjd->wnid', weighted, visitor)
            text_part = jnp.einsum('wnij,wnid->wnjd', weighted, image_half)
            text_grad = text_grad + jnp.roll(text_part, (-offsets[0], -offsets[1]), axis=(0, 1))
    grad_images = unit_backward(image_unit, image_inverse, image_grad.reshape(BATCH, D))
    grad_texts = unit_backward(text_unit, text_inverse, text_grad.reshape(BATCH, D))
    return (grad_images, grad_texts)
```

```python
import functools

import jax
import jax.numpy as jnp
from jax import lax
from jax.experimental import pallas as pl
from jax.experimental.pallas import tpu as pltpu
from jax.sharding import PartitionSpec as P

EPS = 1e-06
AXES = ("wide", "narrow")
NT = (((1,), (1,)), ((), ()))
NN = (((1,), (0,)), ((), ()))
TN = (((0,), (0,)), ((), ()))
VMEM_LIMIT = 48 * 1024 * 1024
F32 = jnp.float32
BF16 = jnp.bfloat16


def mm(a, b, dims):
    return lax.dot_general(a, b, dims, preferred_element_type=F32)


def whole(space=pltpu.VMEM):
    return pl.BlockSpec(memory_space=space)


def unit_of(rows):
    floats = rows.astype(F32)
    inverse = lax.rsqrt(jnp.sum(floats * floats, axis=-1, keepdims=True) + EPS)
    return floats * inverse, inverse


def weights(scores, temper, offset):
    return (temper * jax.nn.sigmoid(temper * scores + offset)).astype(BF16)


def call(kernel, outs, inputs, matmuls, aliases=None):
    specs = [whole(pltpu.SMEM if x.ndim == 1 else pltpu.VMEM) for x in inputs]
    moved = sum(x.size * x.dtype.itemsize for x in inputs)
    moved += sum(x.size * x.dtype.itemsize for x in outs)
    return pl.pallas_call(
        kernel,
        out_shape=outs,
        in_specs=specs,
        out_specs=[whole() for _ in outs],
        input_output_aliases=aliases or {},
        compiler_params=pltpu.CompilerParams(vmem_limit_bytes=VMEM_LIMIT),
        cost_estimate=pl.CostEstimate(
            flops=matmuls * 2 * 256 * 256 * 1152, bytes_accessed=moved, transcendentals=0
        ),
    )(*inputs)


def prepare_kernel(texts, images, text_half, image_half, both):
    rows = texts.shape[0]
    half = unit_of(texts[...])[0].astype(BF16)
    text_half[...] = half
    both[:rows] = half
    half = unit_of(images[...])[0].astype(BF16)
    image_half[...] = half
    both[rows:] = half


def own_kernel(
    temper, flags, labels, text_half, image_half, text_other, image_other,
    image_own, image_far, text_own, text_far,
):
    scale, offset = temper[0], temper[1]
    text, image = text_half[...], image_half[...]
    scores = mm(image, text, NT)
    target = lax.broadcasted_iota(jnp.int32, scores.shape, 1)
    positive = (labels[...] == target).astype(F32)
    residual = jax.nn.sigmoid(scale * scores + offset) - positive
    weighted = (scale * residual).astype(BF16)
    image_own[...] = mm(weighted, text, NN)
    text_own[...] = mm(weighted, image, TN)

    @pl.when(flags[0] == 0)
    def _():
        part = weights(mm(image_other[...], text, NT), scale, offset)
        image_far[...] = mm(part, text, NN)
        text_far[...] = jnp.zeros(text_far.shape, F32)

    @pl.when(flags[0] == 1)
    def _():
        part = weights(mm(text_other[...], image, NT), scale, offset)
        text_far[...] = mm(part, image, NN)
        image_far[...] = jnp.zeros(image_far.shape, F32)


def visit_kernel(
    always, temper, flags, visitor, own, other, own_in, far_in, own_out, far_out
):
    scale, offset = temper[0], temper[1]
    block = visitor[...]

    def far():
        part = weights(mm(other[...], block, NT), scale, offset)
        far_out[...] = far_in[...] + mm(part, block, NN)

    if always is None:
        far()
    else:
        pl.when(flags[0] == always)(far)

        @pl.when(flags[0] != always)
        def _():
            far_out[...] = far_in[...]

    part = weights(mm(own[...], block, NT), scale, offset)
    own_out[...] = own_in[...] + mm(part, block, NN)


def last_kernel(temper, visitor, own, rows, own_in, received, grad):
    scale, offset = temper[0], temper[1]
    block = visitor[...]
    part = weights(mm(own[...], block, NT), scale, offset)
    upstream = own_in[...] + received[...] + mm(part, block, NN)
    unit, inverse = unit_of(rows[...])
    along = jnp.sum(unit * upstream, axis=-1, keepdims=True)
    grad[...] = inverse * (upstream - unit * along)


def shards(images, texts, labels, log_scale, bias):
    n_wide, n_narrow = lax.axis_size("wide"), lax.axis_size("narrow")
    wide, narrow = lax.axis_index("wide"), lax.axis_index("narrow")
    rows, width = images.shape
    core = narrow % 2

    def moved(value, place):
        pairs = []
        for w in range(n_wide):
            for n in range(n_narrow):
                a, b = place(w, n)
                pairs.append((w * n_narrow + n, a % n_wide * n_narrow + b % n_narrow))
        return lax.ppermute(value, AXES, pairs)

    def hop(value, sign, w_step, chips):
        return moved(value, lambda w, n: (w + sign * w_step, n + 2 * sign * chips))

    def last_hop(value, sign):
        def place(w, n):
            even = n % 2 == (0 if sign > 0 else 1)
            m = n + 1 - 2 * (n % 2)
            return (w + sign, m) if even else (w, m + 2 * sign)

        return moved(value, place)

    def swapped(value):
        return moved(value, lambda w, n: (w, n + 1 - 2 * (n % 2)))

    temper = jnp.stack([jnp.exp(log_scale[0]), bias[0]])
    flags = core.reshape(1).astype(jnp.int32)
    local = (labels - (wide * n_narrow + narrow) * rows).reshape(rows, 1)
    half = jax.ShapeDtypeStruct((rows, width), BF16)
    full = jax.ShapeDtypeStruct((rows, width), F32)
    pair = jax.ShapeDtypeStruct((2 * rows, width), BF16)

    text_half, image_half, both = call(prepare_kernel, [half, half, pair], [texts, images], 0)
    both = swapped(both)
    a_text, a_image = hop(text_half, 1, 0, 1), hop(image_half, -1, 0, 1)
    d_text, d_image = hop(text_half, 1, 1, 3), hop(image_half, -1, 1, 3)
    text_other, image_other = both[:rows], both[rows:]
    image_own, image_far, text_own, text_far = call(
        own_kernel,
        [full] * 4,
        [temper, flags, local, text_half, image_half, text_other, image_other],
        5,
    )
    b_text, b_image = last_hop(a_text, 1), last_hop(a_image, -1)
    c_text, c_image = hop(d_text, 1, 0, -1), hop(d_image, -1, 0, -1)

    def visit(always, visitor, own, other, own_sum, far_sum):
        return call(
            functools.partial(visit_kernel, always),
            [full, full],
            [temper, flags, visitor, own, other, own_sum, far_sum],
            4,
            {5: 0, 6: 1},
        )

    for always_t, always_i, text, image in (
        (None, None, a_text, a_image),
        (1, 0, d_text, d_image),
        (None, None, c_text, c_image),
    ):
        image_own, image_far = visit(always_t, text, image_half, image_other, image_own, image_far)
        text_own, text_far = visit(always_i, image, text_half, text_other, text_own, text_far)
    image_back, text_back = swapped(image_far), swapped(text_far)
    (grad_images,) = call(
        last_kernel, [full], [temper, b_text, image_half, images, image_own, image_back], 2
    )
    (grad_texts,) = call(
        last_kernel, [full], [temper, b_image, text_half, texts, text_own, text_back], 2
    )
    return (grad_images, grad_texts)


def solution(mesh):
    return jax.shard_map(
        shards,
        mesh=mesh,
        in_specs=(P(AXES, None), P(AXES, None), P(AXES), P(), P()),
        out_specs=(P(AXES, None), P(AXES, None)),
        check_vma=False,
    )
```

```python
import functools

import jax
import jax.numpy as jnp
from jax import lax
from jax.experimental import pallas as pl
from jax.experimental.pallas import tpu as pltpu
from jax.sharding import PartitionSpec as P

EPS = 1e-06
AXES = ("wide", "narrow")
NT = (((1,), (1,)), ((), ()))
NN = (((1,), (0,)), ((), ()))
TN = (((0,), (0,)), ((), ()))
VMEM_LIMIT = 48 * 1024 * 1024
F32 = jnp.float32
BF16 = jnp.bfloat16


def mm(a, b, dims):
    return lax.dot_general(a, b, dims, preferred_element_type=F32)


def whole(space=pltpu.VMEM):
    return pl.BlockSpec(memory_space=space)


def unit_of(rows):
    floats = rows.astype(F32)
    inverse = lax.rsqrt(jnp.sum(floats * floats, axis=-1, keepdims=True) + EPS)
    return floats * inverse, inverse


def weights(scores, temper, offset):
    return (temper * jax.nn.sigmoid(temper * scores + offset)).astype(BF16)


def call(kernel, outs, inputs, aliases=None, passed=()):
    specs = [whole(pltpu.SMEM if x.ndim == 1 else pltpu.VMEM) for x in inputs]
    out_specs = [whole() for _ in outs]
    for source, target in passed:
        specs[source] = whole(pl.ANY)
        if target is not None:
            out_specs[target] = whole(pl.ANY)
    return pl.pallas_call(
        kernel,
        out_shape=outs,
        in_specs=specs,
        out_specs=out_specs,
        input_output_aliases=aliases or {},
        compiler_params=pltpu.CompilerParams(vmem_limit_bytes=VMEM_LIMIT),
        cost_estimate=pl.CostEstimate(flops=1000, bytes_accessed=1000, transcendentals=0),
    )(*inputs)


def prepare_kernel(texts, images, text_half, image_half, both):
    rows = texts.shape[0]
    half = unit_of(texts[...])[0].astype(BF16)
    text_half[...] = half
    both[:rows] = half
    half = unit_of(images[...])[0].astype(BF16)
    image_half[...] = half
    both[rows:] = half


def own_kernel(
    temper, flags, labels, text_half, image_half, other,
    image_own, image_far, text_own, text_far,
):
    scale, offset = temper[0], temper[1]
    rows = text_half.shape[0]
    text, image = text_half[...], image_half[...]
    scores = mm(image, text, NT)
    target = lax.broadcasted_iota(jnp.int32, scores.shape, 1)
    positive = (labels[...] == target).astype(F32)
    residual = jax.nn.sigmoid(scale * scores + offset) - positive
    weighted = (scale * residual).astype(BF16)
    image_own[...] = mm(weighted, text, NN)
    text_own[...] = mm(weighted, image, TN)

    @pl.when(flags[0] == 0)
    def _():
        part = weights(mm(other[rows:], text, NT), scale, offset)
        image_far[...] = mm(part, text, NN)
        text_far[...] = jnp.zeros(text_far.shape, F32)

    @pl.when(flags[0] == 1)
    def _():
        part = weights(mm(other[:rows], image, NT), scale, offset)
        text_far[...] = mm(part, image, NN)
        image_far[...] = jnp.zeros(image_far.shape, F32)


def visit_kernel(
    only, first, temper, flags, visitor, own, other, own_in, far_in, own_out, far_out
):
    scale, offset = temper[0], temper[1]
    rows = visitor.shape[0]
    block = unit_of(visitor[...])[0].astype(BF16)

    def far():
        part = weights(mm(other[first : first + rows], block, NT), scale, offset)
        far_out[...] = far_in[...] + mm(part, block, NN)

    if only is None:
        far()
    else:
        pl.when(flags[0] == only)(far)

        @pl.when(flags[0] != only)
        def _():
            far_out[...] = far_in[...]

    part = weights(mm(own[...], block, NT), scale, offset)
    own_out[...] = own_in[...] + mm(part, block, NN)


def far_kernel(first, temper, visitor, other, far_in, half, far_out):
    rows = visitor.shape[0]
    block = unit_of(visitor[...])[0].astype(BF16)
    half[...] = block
    part = weights(mm(other[first : first + rows], block, NT), temper[0], temper[1])
    far_out[...] = far_in[...] + mm(part, block, NN)


def near_kernel(raw, temper, visitor, own, own_in, *rest):
    own_out = rest[-1] if len(rest) == 1 else rest[1]
    block = visitor[...]
    if raw:
        block = unit_of(block)[0].astype(BF16)
    part = weights(mm(own[...], block, NT), temper[0], temper[1])
    own_out[...] = own_in[...] + mm(part, block, NN)


def finish_kernel(rows, own_sum, received, grad):
    upstream = own_sum[...] + received[...]
    unit, inverse = unit_of(rows[...])
    along = jnp.sum(unit * upstream, axis=-1, keepdims=True)
    grad[...] = inverse * (upstream - unit * along)


def shards(images, texts, labels, log_scale, bias):
    n_wide, n_narrow = lax.axis_size("wide"), lax.axis_size("narrow")
    wide, narrow = lax.axis_index("wide"), lax.axis_index("narrow")
    rows, width = images.shape
    core = narrow % 2

    def moved(value, place):
        pairs = []
        for w in range(n_wide):
            for n in range(n_narrow):
                a, b = place(w, n)
                pairs.append((w * n_narrow + n, a % n_wide * n_narrow + b % n_narrow))
        return lax.ppermute(value, AXES, pairs)

    def hop(value, sign, w_step, chips):
        return moved(value, lambda w, n: (w + sign * w_step, n + 2 * sign * chips))

    def last_hop(value, sign):
        def place(w, n):
            even = n % 2 == (0 if sign > 0 else 1)
            m = n + 1 - 2 * (n % 2)
            return (w + sign, m) if even else (w, m + 2 * sign)

        return moved(value, place)

    def swapped(value):
        return moved(value, lambda w, n: (w, n + 1 - 2 * (n % 2)))

    temper = jnp.stack([jnp.exp(log_scale[0]), bias[0]])
    flags = core.reshape(1).astype(jnp.int32)
    local = (labels - (wide * n_narrow + narrow) * rows).reshape(rows, 1)
    half = jax.ShapeDtypeStruct((rows, width), BF16)
    full = jax.ShapeDtypeStruct((rows, width), F32)
    pair = jax.ShapeDtypeStruct((2 * rows, width), BF16)

    a_text, a_image = hop(texts, 1, 0, 1), hop(images, -1, 0, 1)
    d_text, d_image = hop(texts, 1, 1, 3), hop(images, -1, 1, 3)
    text_half, image_half, both = call(
        prepare_kernel, [half, half, pair], [texts, images]
    )
    other = swapped(both)
    b_text, b_image = last_hop(a_text, 1), last_hop(a_image, -1)
    c_text, c_image = hop(d_text, 1, 0, -1), hop(d_image, -1, 0, -1)

    image_own, image_far, text_own, text_far = call(
        own_kernel, [full] * 4, [temper, flags, local, text_half, image_half, other]
    )

    def visit(only, first, visitor, own, own_sum, far_sum):
        return call(
            functools.partial(visit_kernel, only, first),
            [full, full],
            [temper, flags, visitor, own, other, own_sum, far_sum],
            {5: 0, 6: 1},
        )

    def far(first, visitor, far_sum):
        return call(
            functools.partial(far_kernel, first),
            [half, full],
            [temper, visitor, other, far_sum],
            {3: 1},
        )

    def near(raw, visitor, own, own_sum, later=None):
        inputs = [temper, visitor, own, own_sum]
        kernel = functools.partial(near_kernel, raw)
        if later is None:
            return call(kernel, [full], inputs, {3: 0})[0]
        return call(kernel, [full, full], inputs + [later], {3: 0, 4: 1}, ((4, 1),))

    for only_t, only_i, text, image in (
        (None, None, a_text, a_image),
        (1, 0, d_text, d_image),
    ):
        image_own, image_far = visit(only_t, rows, text, image_half, image_own, image_far)
        text_own, text_far = visit(only_i, 0, image, text_half, text_own, text_far)
    image_own, image_far = near(True, b_text, image_half, image_own, image_far)
    text_own, text_far = near(True, b_image, text_half, text_own, text_far)
    c_text, image_far = far(rows, c_text, image_far)
    image_back = swapped(image_far)
    c_image, text_far = far(0, c_image, text_far)
    text_back = swapped(text_far)
    image_own = near(False, c_text, image_half, image_own)
    text_own = near(False, c_image, text_half, text_own)
    (grad_images,) = call(finish_kernel, [full], [images, image_own, image_back])
    (grad_texts,) = call(finish_kernel, [full], [texts, text_own, text_back])
    return (grad_images, grad_texts)


def solution(mesh):
    return jax.shard_map(
        shards,
        mesh=mesh,
        in_specs=(P(AXES, None), P(AXES, None), P(AXES), P(), P()),
        out_specs=(P(AXES, None), P(AXES, None)),
        check_vma=False,
    )
```

```python
import functools

import jax
import jax.numpy as jnp
from jax import lax
from jax.experimental import pallas as pl
from jax.experimental.pallas import tpu as pltpu
from jax.sharding import PartitionSpec as P

EPS = 1e-06
AXES = ("wide", "narrow")
NT = (((1,), (1,)), ((), ()))
NN = (((1,), (0,)), ((), ()))
VMEM_LIMIT = 48 * 1024 * 1024
F32 = jnp.float32
BF16 = jnp.bfloat16


def mm(a, b, dims):
    return lax.dot_general(a, b, dims, preferred_element_type=F32)


def unit_of(rows):
    floats = rows.astype(F32)
    inverse = lax.rsqrt(jnp.sum(floats * floats, axis=-1, keepdims=True) + EPS)
    return floats * inverse, inverse


def half_of(rows):
    return unit_of(rows)[0].astype(BF16)


def call(kernel, outs, inputs, scratch=(), aliases=None):
    specs = [
        pl.BlockSpec(memory_space=pltpu.SMEM if x.ndim == 1 else pltpu.VMEM) for x in inputs
    ]
    return pl.pallas_call(
        kernel,
        out_shape=outs,
        in_specs=specs,
        out_specs=[pl.BlockSpec(memory_space=pltpu.VMEM) for _ in outs],
        scratch_shapes=list(scratch),
        input_output_aliases=aliases or {},
        compiler_params=pltpu.CompilerParams(vmem_limit_bytes=VMEM_LIMIT),
        cost_estimate=pl.CostEstimate(flops=1000, bytes_accessed=1000, transcendentals=0),
    )(*inputs)


def weigh(temper, resident, visitors, first, weighted, count, positive=None):
    scale, offset = temper[0], temper[1]
    rows = resident.shape[0]
    for k in range(count):
        block = visitors[pl.ds(pl.multiple_of(first + k * rows, rows), rows), :]
        scores = mm(resident, block, NT)
        residual = jax.nn.sigmoid(scale * scores + offset)
        if k == 0 and positive is not None:
            residual = residual - positive
        weighted[:, k * rows : (k + 1) * rows] = (scale * residual).astype(BF16)


def gather(weighted, visitors, first, count, out, before=None):
    rows, width = out.shape
    step = width // 3
    left = weighted[:, : count * rows]
    for at in range(0, width, step):
        block = visitors[pl.ds(pl.multiple_of(first, rows), count * rows), at : at + step]
        part = mm(left, block, NN)
        if before is not None:
            part = before[:, at : at + step] + part
        out[:, at : at + step] = part


def early_kernel(
    temper, flags, column, row, texts, images, other,
    a_text, a_image, d_text, d_image,
    text_half, image_half, text_other, image_other,
    image_near, image_far, text_near, text_far,
    texts_met, images_met, image_weights, image_far_weights, text_weights, text_far_weights,
):
    rows = texts.shape[0]
    square = (rows, rows)
    text, image = half_of(texts[...]), half_of(images[...])
    text_half[...] = text
    image_half[...] = image
    text_other[...] = half_of(other[:rows])
    image_other[...] = half_of(other[rows:])

    def stream(core, own, one, three, near, far, positive, near_sum, far_sum, visitors, *tables):
        visitors[:rows] = own
        visitors[rows : 2 * rows] = half_of(one[...])
        visitors[2 * rows :] = half_of(three[...])
        weigh(temper, near, visitors, 0, tables[0], 3, positive.astype(F32))
        gather(tables[0], visitors, 0, 3, near_sum)
        first = core * rows
        weigh(temper, far, visitors, first, tables[1], 2)
        gather(tables[1], visitors, first, 2, far_sum)

    target = lax.broadcasted_iota(jnp.int32, square, 1)
    stream(
        flags[0], text, a_text, d_text, image, image_other[...],
        column[...] == target, image_near, image_far,
        texts_met, image_weights, image_far_weights,
    )
    target = lax.broadcasted_iota(jnp.int32, square, 0)
    stream(
        1 - flags[0], image, a_image, d_image, text, text_other[...],
        row[...] == target, text_near, text_far,
        images_met, text_weights, text_far_weights,
    )


def far_kernel(temper, c_block, other, far_in, half, far_out, weighted):
    half[...] = half_of(c_block[...])
    weigh(temper, other[...], half, 0, weighted, 1)
    gather(weighted, half, 0, 1, far_out, far_in)


def near_kernel(
    temper, b_text, c_text, image_half, image_in, b_image, c_image, text_half, text_in,
    image_out, text_out, texts_met, images_met, image_weights, text_weights,
):
    rows = b_text.shape[0]
    for last, half, own, before, out, visitors, weighted in (
        (b_text, c_text, image_half, image_in, image_out, texts_met, image_weights),
        (b_image, c_image, text_half, text_in, text_out, images_met, text_weights),
    ):
        visitors[:rows] = half_of(last[...])
        visitors[rows:] = half[...]
        weigh(temper, own[...], visitors, 0, weighted, 2)
        gather(weighted, visitors, 0, 2, out, before)


def finish_kernel(rows, near, received, grad):
    upstream = near[...] + received[...]
    unit, inverse = unit_of(rows[...])
    along = jnp.sum(unit * upstream, axis=-1, keepdims=True)
    grad[...] = inverse * (upstream - unit * along)


def shards(images, texts, labels, log_scale, bias):
    n_wide, n_narrow = lax.axis_size("wide"), lax.axis_size("narrow")
    wide, narrow = lax.axis_index("wide"), lax.axis_index("narrow")
    rows, width = images.shape
    core = narrow % 2

    def moved(value, place):
        pairs = []
        for w in range(n_wide):
            for n in range(n_narrow):
                a, b = place(w, n)
                pairs.append((w * n_narrow + n, a % n_wide * n_narrow + b % n_narrow))
        return lax.ppermute(value, AXES, pairs)

    def hop(value, sign, w_step, chips):
        return moved(value, lambda w, n: (w + sign * w_step, n + 2 * sign * chips))

    def last_hop(value, sign):
        def place(w, n):
            even = n % 2 == (0 if sign > 0 else 1)
            m = n + 1 - 2 * (n % 2)
            return (w + sign, m) if even else (w, m + 2 * sign)

        return moved(value, place)

    def swapped(value):
        return moved(value, lambda w, n: (w, n + 1 - 2 * (n % 2)))

    temper = jnp.stack([jnp.exp(log_scale[0]), bias[0]])
    flags = core.reshape(1).astype(jnp.int32)
    local = labels - (wide * n_narrow + narrow) * rows
    half = jax.ShapeDtypeStruct((rows, width), BF16)
    full = jax.ShapeDtypeStruct((rows, width), F32)

    def table(kind, blocks):
        shape = (blocks * rows, width) if kind == "v" else (rows, blocks * rows)
        return pltpu.VMEM(shape, BF16)

    a_text, a_image = hop(texts, 1, 0, 1), hop(images, -1, 0, 1)
    d_text, d_image = hop(texts, 1, 1, 3), hop(images, -1, 1, 3)
    other = swapped(jnp.concatenate([texts, images]))
    a_text, a_image, other = lax.optimization_barrier((a_text, a_image, other))
    b_text, b_image = last_hop(a_text, 1), last_hop(a_image, -1)
    d_text, d_image = lax.optimization_barrier((d_text, d_image))
    c_text, c_image = hop(d_text, 1, 0, -1), hop(d_image, -1, 0, -1)

    (text_half, image_half, text_other, image_other, image_near, image_far, text_near, text_far) = (
        call(
            early_kernel,
            [half] * 4 + [full] * 4,
            [
                temper, flags, local.reshape(rows, 1), local.reshape(1, rows),
                texts, images, other, a_text, a_image, d_text, d_image,
            ],
            [table("v", 3)] * 2 + [table("w", 3), table("w", 2)] * 2,
        )
    )

    def far(block, other, far_sum):
        return call(
            far_kernel, [half, full], [temper, block, other, far_sum], [table("w", 1)], {3: 1}
        )

    b_text, b_image, image_far, text_far = lax.optimization_barrier(
        (b_text, b_image, image_far, text_far)
    )
    c_text, image_far = far(c_text, image_other, image_far)
    image_back = swapped(image_far)
    c_image, text_far = far(c_image, text_other, text_far)
    text_back = swapped(text_far)
    image_near, text_near = call(
        near_kernel,
        [full, full],
        [temper, b_text, c_text, image_half, image_near, b_image, c_image, text_half, text_near],
        [table("v", 2)] * 2 + [table("w", 2)] * 2,
        {4: 0, 8: 1},
    )
    (grad_images,) = call(finish_kernel, [full], [images, image_near, image_back])
    (grad_texts,) = call(finish_kernel, [full], [texts, text_near, text_back])
    return (grad_images, grad_texts)


def solution(mesh):
    return jax.shard_map(
        shards,
        mesh=mesh,
        in_specs=(P(AXES, None), P(AXES, None), P(AXES), P(), P()),
        out_specs=(P(AXES, None), P(AXES, None)),
        check_vma=False,
    )
```

```python
import functools

import jax
import jax.numpy as jnp
from jax import lax
from jax.experimental import pallas as pl
from jax.experimental.pallas import tpu as pltpu
from jax.sharding import PartitionSpec as P

EPS = 1e-06
AXES = ("wide", "narrow")
NT = (((1,), (1,)), ((), ()))
NN = (((1,), (0,)), ((), ()))
VMEM_LIMIT = 20 * 1024 * 1024
F32 = jnp.float32
BF16 = jnp.bfloat16


def mm(a, b, dims):
    return lax.dot_general(a, b, dims, preferred_element_type=F32)


def unit_of(rows):
    floats = rows.astype(F32)
    inverse = lax.rsqrt(jnp.sum(floats * floats, axis=-1, keepdims=True) + EPS)
    return floats * inverse, inverse


def half_of(rows):
    return unit_of(rows)[0].astype(BF16)


def call(kernel, outs, inputs, aliases=None):
    specs = [
        pl.BlockSpec(memory_space=pltpu.SMEM if x.ndim == 1 else pltpu.VMEM) for x in inputs
    ]
    return pl.pallas_call(
        kernel,
        out_shape=outs,
        in_specs=specs,
        out_specs=[pl.BlockSpec(memory_space=pltpu.VMEM) for _ in outs],
        input_output_aliases=aliases or {},
        compiler_params=pltpu.CompilerParams(vmem_limit_bytes=VMEM_LIMIT),
        cost_estimate=pl.CostEstimate(flops=1000, bytes_accessed=1000, transcendentals=0),
    )(*inputs)


def weigh(temper, resident, block, positive=None):
    scale, offset = temper[0], temper[1]
    residual = jax.nn.sigmoid(scale * mm(resident, block, NT) + offset)
    if positive is not None:
        residual = residual - positive.astype(F32)
    return (scale * residual).astype(BF16)


def own_kernel(
    temper, flags, column, row, texts, images, other,
    text_half, image_half, text_other, image_other,
    image_near, image_far, text_near, text_far,
):
    rows = texts.shape[0]
    text, image = half_of(texts[...]), half_of(images[...])
    text_half[...] = text
    image_half[...] = image
    text_other[...] = half_of(other[:rows])
    image_other[...] = half_of(other[rows:])
    target = lax.broadcasted_iota(jnp.int32, (rows, rows), 1)
    image_near[...] = mm(weigh(temper, image, text, column[...] == target), text, NN)
    target = lax.broadcasted_iota(jnp.int32, (rows, rows), 0)
    text_near[...] = mm(weigh(temper, text, image, row[...] == target), image, NN)

    @pl.when(flags[0] == 0)
    def _():
        image_far[...] = mm(weigh(temper, image_other[...], text), text, NN)
        text_far[...] = jnp.zeros(text_far.shape, F32)

    @pl.when(flags[0] == 1)
    def _():
        text_far[...] = mm(weigh(temper, text_other[...], image), image, NN)
        image_far[...] = jnp.zeros(image_far.shape, F32)


def both_kernel(
    temper, text, image, image_half, image_other, text_half, text_other,
    image_near_in, image_far_in, text_near_in, text_far_in,
    image_near, image_far, text_near, text_far,
):
    for visitor, own, other, near_in, far_in, near, far in (
        (text, image_half, image_other, image_near_in, image_far_in, image_near, image_far),
        (image, text_half, text_other, text_near_in, text_far_in, text_near, text_far),
    ):
        block = half_of(visitor[...])
        near[...] = near_in[...] + mm(weigh(temper, own[...], block), block, NN)
        far[...] = far_in[...] + mm(weigh(temper, other[...], block), block, NN)


def side_kernel(
    temper, flags, d_text, d_image, b_text, b_image,
    image_half, image_other, text_half, text_other,
    image_near_in, image_far_in, text_near_in, text_far_in,
    image_near, image_far, text_near, text_far,
):
    for core, three, last, own, other, near_in, far_in, near, far in (
        (1, d_text, b_text, image_half, image_other,
         image_near_in, image_far_in, image_near, image_far),
        (0, d_image, b_image, text_half, text_other,
         text_near_in, text_far_in, text_near, text_far),
    ):
        block, final = half_of(three[...]), half_of(last[...])
        part = mm(weigh(temper, own[...], block), block, NN)
        near[...] = near_in[...] + part + mm(weigh(temper, own[...], final), final, NN)

        @pl.when(flags[0] == core)
        def _():
            far[...] = far_in[...] + mm(weigh(temper, other[...], block), block, NN)

        @pl.when(flags[0] != core)
        def _():
            far[...] = far_in[...]


def far_kernel(temper, c_block, other, far_in, half, far):
    block = half_of(c_block[...])
    half[...] = block
    far[...] = far_in[...] + mm(weigh(temper, other[...], block), block, NN)


def near_kernel(
    temper, c_text, image_half, image_in, c_image, text_half, text_in, image_out, text_out
):
    for visitor, own, before, out in (
        (c_text, image_half, image_in, image_out),
        (c_image, text_half, text_in, text_out),
    ):
        block = visitor[...]
        out[...] = before[...] + mm(weigh(temper, own[...], block), block, NN)


def finish_kernel(rows, near, received, grad):
    upstream = near[...] + received[...]
    unit, inverse = unit_of(rows[...])
    along = jnp.sum(unit * upstream, axis=-1, keepdims=True)
    grad[...] = inverse * (upstream - unit * along)


def shards(images, texts, labels, log_scale, bias):
    n_wide, n_narrow = lax.axis_size("wide"), lax.axis_size("narrow")
    wide, narrow = lax.axis_index("wide"), lax.axis_index("narrow")
    rows, width = images.shape
    core = narrow % 2

    def moved(value, place):
        pairs = []
        for w in range(n_wide):
            for n in range(n_narrow):
                a, b = place(w, n)
                pairs.append((w * n_narrow + n, a % n_wide * n_narrow + b % n_narrow))
        return lax.ppermute(value, AXES, pairs)

    def hop(value, sign, w_step, chips):
        return moved(value, lambda w, n: (w + sign * w_step, n + 2 * sign * chips))

    def last_hop(value, sign):
        def place(w, n):
            even = n % 2 == (0 if sign > 0 else 1)
            m = n + 1 - 2 * (n % 2)
            return (w + sign, m) if even else (w, m + 2 * sign)

        return moved(value, place)

    def swapped(value):
        return moved(value, lambda w, n: (w, n + 1 - 2 * (n % 2)))

    temper = jnp.stack([jnp.exp(log_scale[0]), bias[0]])
    flags = core.reshape(1).astype(jnp.int32)
    local = labels - (wide * n_narrow + narrow) * rows
    half = jax.ShapeDtypeStruct((rows, width), BF16)
    full = jax.ShapeDtypeStruct((rows, width), F32)

    a_text, a_image = hop(texts, 1, 0, 1), hop(images, -1, 0, 1)
    d_text, d_image = hop(texts, 1, 1, 3), hop(images, -1, 1, 3)
    other = swapped(jnp.concatenate([texts, images]))

    (text_half, image_half, text_other, image_other, *sums) = call(
        own_kernel,
        [half] * 4 + [full] * 4,
        [temper, flags, local.reshape(rows, 1), local.reshape(1, rows), texts, images, other],
    )
    residents = [image_half, image_other, text_half, text_other]
    a_text, a_image, *sums = lax.optimization_barrier((a_text, a_image, *sums))
    b_text, b_image = last_hop(a_text, 1), last_hop(a_image, -1)
    sums = call(
        both_kernel,
        [full] * 4,
        [temper, a_text, a_image, *residents, *sums],
        {7: 0, 8: 1, 9: 2, 10: 3},
    )
    d_text, d_image, *sums = lax.optimization_barrier((d_text, d_image, *sums))
    c_text, c_image = hop(d_text, 1, 0, -1), hop(d_image, -1, 0, -1)
    image_near, image_far, text_near, text_far = call(
        side_kernel,
        [full] * 4,
        [temper, flags, d_text, d_image, b_text, b_image, *residents, *sums],
        {10: 0, 11: 1, 12: 2, 13: 3},
    )

    def far(block, other, far_sum):
        return call(far_kernel, [half, full], [temper, block, other, far_sum], {3: 1})

    c_text, image_far = far(c_text, image_other, image_far)
    image_back = swapped(image_far)
    c_image, text_far = far(c_image, text_other, text_far)
    text_back = swapped(text_far)
    image_near, text_near = call(
        near_kernel,
        [full, full],
        [temper, c_text, image_half, image_near, c_image, text_half, text_near],
        {3: 0, 6: 1},
    )
    (grad_images,) = call(finish_kernel, [full], [images, image_near, image_back])
    (grad_texts,) = call(finish_kernel, [full], [texts, text_near, text_back])
    return (grad_images, grad_texts)


def solution(mesh):
    return jax.shard_map(
        shards,
        mesh=mesh,
        in_specs=(P(AXES, None), P(AXES, None), P(AXES), P(), P()),
        out_specs=(P(AXES, None), P(AXES, None)),
        check_vma=False,
    )
```

```python
import functools

import jax
import jax.numpy as jnp
from jax import lax
from jax.experimental import pallas as pl
from jax.experimental.pallas import tpu as pltpu
from jax.sharding import PartitionSpec as P

EPS = 1e-06
AXES = ("wide", "narrow")
NT = (((1,), (1,)), ((), ()))
NN = (((1,), (0,)), ((), ()))
VMEM_LIMIT = 20 * 1024 * 1024
F32 = jnp.float32
BF16 = jnp.bfloat16


def mm(a, b, dims):
    return lax.dot_general(a, b, dims, preferred_element_type=F32)


def unit_of(rows):
    floats = rows.astype(F32)
    inverse = lax.rsqrt(jnp.sum(floats * floats, axis=-1, keepdims=True) + EPS)
    return floats * inverse, inverse


def half_of(rows):
    return unit_of(rows)[0].astype(BF16)


def call(kernel, outs, inputs, aliases=None):
    specs = [
        pl.BlockSpec(memory_space=pltpu.SMEM if x.ndim == 1 else pltpu.VMEM) for x in inputs
    ]
    return pl.pallas_call(
        kernel,
        out_shape=outs,
        in_specs=specs,
        out_specs=[pl.BlockSpec(memory_space=pltpu.VMEM) for _ in outs],
        input_output_aliases=aliases or {},
        compiler_params=pltpu.CompilerParams(vmem_limit_bytes=VMEM_LIMIT),
        cost_estimate=pl.CostEstimate(flops=1000, bytes_accessed=1000, transcendentals=0),
    )(*inputs)


def weigh(temper, resident, block, positive=None):
    scale, offset = temper[0], temper[1]
    residual = jax.nn.sigmoid(scale * mm(resident, block, NT) + offset)
    if positive is not None:
        residual = residual - positive.astype(F32)
    return (scale * residual).astype(BF16)


def own_kernel(
    temper, flags, column, row, texts, images, other,
    text_half, image_half, text_other, image_other,
    image_near, image_far, text_near, text_far,
):
    rows = texts.shape[0]
    text, image = half_of(texts[...]), half_of(images[...])
    text_half[...] = text
    image_half[...] = image
    text_other[...] = half_of(other[:rows])
    image_other[...] = half_of(other[rows:])
    target = lax.broadcasted_iota(jnp.int32, (rows, rows), 1)
    image_near[...] = mm(weigh(temper, image, text, column[...] == target), text, NN)
    target = lax.broadcasted_iota(jnp.int32, (rows, rows), 0)
    text_near[...] = mm(weigh(temper, text, image, row[...] == target), image, NN)

    @pl.when(flags[0] == 0)
    def _():
        image_far[...] = mm(weigh(temper, image_other[...], text), text, NN)
        text_far[...] = jnp.zeros(text_far.shape, F32)

    @pl.when(flags[0] == 1)
    def _():
        text_far[...] = mm(weigh(temper, text_other[...], image), image, NN)
        image_far[...] = jnp.zeros(image_far.shape, F32)


def meet(wanted, temper, resident, block, before, after):
    @pl.when(wanted != 0)
    def _():
        after[...] = before[...] + mm(weigh(temper, resident[...], block), block, NN)

    @pl.when(wanted == 0)
    def _():
        after[...] = before[...]


def visit_kernel(
    temper, flags, text, image, image_half, image_other, text_half, text_other,
    image_near_in, image_far_in, text_near_in, text_far_in,
    image_near, image_far, text_near, text_far,
):
    for k, visitor, near_res, far_res, near_in, far_in, near, far in (
        (0, text, image_half, image_other, image_near_in, image_far_in, image_near, image_far),
        (2, image, text_half, text_other, text_near_in, text_far_in, text_near, text_far),
    ):
        block = half_of(visitor[...])
        meet(flags[k], temper, near_res, block, near_in, near)
        meet(flags[k + 1], temper, far_res, block, far_in, far)


def far_kernel(k, temper, flags, visitor, far_res, far_in, half, far):
    block = half_of(visitor[...])
    half[...] = block
    meet(flags[k + 1], temper, far_res, block, far_in, far)


def near_kernel(
    temper, flags, text, image_half, image_in, image, text_half, text_in, image_out, text_out
):
    meet(flags[0], temper, image_half, text[...], image_in, image_out)
    meet(flags[2], temper, text_half, image[...], text_in, text_out)


def finish_kernel(rows, near, received, grad):
    upstream = near[...] + received[...]
    unit, inverse = unit_of(rows[...])
    along = jnp.sum(unit * upstream, axis=-1, keepdims=True)
    grad[...] = inverse * (upstream - unit * along)


STEPS = ({"A": (0, 1), "B": (1, 1), "C": (1, 2), "D": (1, 3)},
         {"A": (0, 1), "B": (0, 2), "C": (1, 2), "D": (1, 3)})
MEETS = ({"A": (1, 1), "B": (0, 1), "C": (1, 1), "D": (1, 0)},
         {"A": (1, 1), "B": (0, 1), "C": (1, 1), "D": (1, 1)})
PLAN = ("DACB", "ADBC")


def plan_of(chip, parity):
    return PLAN[parity]


def hops_of(n_wide, n_narrow):
    chips = n_narrow // 2
    pairs, kinds = [], []
    for k in range(4):
        moves, kind = {}, {}
        for w in range(n_wide):
            for n in range(n_narrow):
                chip, parity = n // 2, n % 2
                plan, steps = plan_of(chip, parity), STEPS[parity]
                before = (0, 0) if k < 2 else steps[plan[k - 2]]
                place = [
                    ((w + a) % n_wide, ((chip + b) % chips) * 2 + parity)
                    for a, b in (before, steps[plan[k]])
                ]
                moves[place[0]] = place[1]
                kind[place[1][1]] = plan[k]
        assert len(moves) == len(set(moves.values())) == n_wide * n_narrow
        pairs.append(moves)
        kinds.append([kind[n] for n in range(n_narrow)])
    return pairs, kinds


def shards(images, texts, labels, log_scale, bias):
    n_wide, n_narrow = lax.axis_size("wide"), lax.axis_size("narrow")
    wide, narrow = lax.axis_index("wide"), lax.axis_index("narrow")
    rows, width = images.shape
    core = narrow % 2
    pairs, kinds = hops_of(n_wide, n_narrow)

    def moved(value, moves):
        flat = [(a * n_narrow + b, c * n_narrow + d) for (a, b), (c, d) in sorted(moves.items())]
        return lax.ppermute(value, AXES, flat)

    def mirrored(moves):
        def turn(place):
            return ((-place[0]) % n_wide, n_narrow - 1 - place[1])

        return {turn(a): turn(b) for a, b in moves.items()}

    def hop(k, text, image):
        return moved(text, pairs[k]), moved(image, mirrored(pairs[k]))

    def swapped(value):
        return moved(
            value,
            {(w, n): (w, n + 1 - 2 * (n % 2)) for w in range(n_wide) for n in range(n_narrow)},
        )

    def flags_of(k):
        table = []
        for n in range(n_narrow):
            m = n_narrow - 1 - n
            line = [*MEETS[n % 2][kinds[k][n]], *MEETS[m % 2][kinds[k][m]]]
            table.append(line)
        return jnp.asarray(table, jnp.int32)[narrow]

    temper = jnp.stack([jnp.exp(log_scale[0]), bias[0]])
    local = labels - (wide * n_narrow + narrow) * rows
    half = jax.ShapeDtypeStruct((rows, width), BF16)
    full = jax.ShapeDtypeStruct((rows, width), F32)

    first = hop(0, texts, images)
    second = hop(1, texts, images)
    other = swapped(jnp.concatenate([texts, images]))
    flags = core.reshape(1).astype(jnp.int32)
    (text_half, image_half, text_other, image_other, *sums) = call(
        own_kernel,
        [half] * 4 + [full] * 4,
        [temper, flags, local.reshape(rows, 1), local.reshape(1, rows), texts, images, other],
    )
    residents = [image_half, image_other, text_half, text_other]

    def visit(k, visitors, sums):
        return call(
            visit_kernel,
            [full] * 4,
            [temper, flags_of(k), *visitors, *residents, *sums],
            {8: 0, 9: 1, 10: 2, 11: 3},
        )

    *first, a, b, c, d = lax.optimization_barrier((*first, *sums))
    third = hop(2, *first)
    sums = visit(0, first, [a, b, c, d])
    *second, a, b, c, d = lax.optimization_barrier((*second, *sums))
    fourth = hop(3, *second)
    sums = visit(1, second, [a, b, c, d])
    sums = visit(2, third, sums)
    image_near, image_far, text_near, text_far = sums

    def far(k, visitor, other, far_sum):
        kernel = functools.partial(far_kernel, k)
        return call(
            kernel, [half, full], [temper, flags_of(3), visitor, other, far_sum], {4: 1}
        )

    text, image_far = far(0, fourth[0], image_other, image_far)
    image_back = swapped(image_far)
    image, text_far = far(2, fourth[1], text_other, text_far)
    text_back = swapped(text_far)
    image_near, text_near = call(
        near_kernel,
        [full, full],
        [temper, flags_of(3), text, image_half, image_near, image, text_half, text_near],
        {4: 0, 7: 1},
    )
    (grad_images,) = call(finish_kernel, [full], [images, image_near, image_back])
    (grad_texts,) = call(finish_kernel, [full], [texts, text_near, text_back])
    return (grad_images, grad_texts)


def solution(mesh):
    return jax.shard_map(
        shards,
        mesh=mesh,
        in_specs=(P(AXES, None), P(AXES, None), P(AXES), P(), P()),
        out_specs=(P(AXES, None), P(AXES, None)),
        check_vma=False,
    )
```

```python
import functools

import jax
import jax.numpy as jnp
from jax import lax
from jax.experimental import pallas as pl
from jax.experimental.pallas import tpu as pltpu
from jax.sharding import PartitionSpec as P

EPS = 1e-06
AXES = ("wide", "narrow")
NT = (((1,), (1,)), ((), ()))
NN = (((1,), (0,)), ((), ()))
VMEM_LIMIT = 20 * 1024 * 1024
F32 = jnp.float32
BF16 = jnp.bfloat16


def mm(a, b, dims):
    return lax.dot_general(a, b, dims, preferred_element_type=F32)


def unit_of(rows):
    floats = rows.astype(F32)
    inverse = lax.rsqrt(jnp.sum(floats * floats, axis=-1, keepdims=True) + EPS)
    return floats * inverse, inverse


def half_of(rows):
    return unit_of(rows)[0].astype(BF16)


def call(kernel, outs, inputs, aliases=None):
    specs = [
        pl.BlockSpec(memory_space=pltpu.SMEM if x.ndim == 1 else pltpu.VMEM) for x in inputs
    ]
    return pl.pallas_call(
        kernel,
        out_shape=outs,
        in_specs=specs,
        out_specs=[pl.BlockSpec(memory_space=pltpu.VMEM) for _ in outs],
        input_output_aliases=aliases or {},
        compiler_params=pltpu.CompilerParams(vmem_limit_bytes=VMEM_LIMIT),
        cost_estimate=pl.CostEstimate(flops=1000, bytes_accessed=1000, transcendentals=0),
    )(*inputs)


def weigh(temper, resident, block, positive=None):
    scale, offset = temper[0], temper[1]
    residual = jax.nn.sigmoid(scale * mm(resident, block, NT) + offset)
    if positive is not None:
        residual = residual - positive.astype(F32)
    return (scale * residual).astype(BF16)


def join_kernel(texts, images, both, semaphores):
    rows = texts.shape[0]
    copies = [
        pltpu.make_async_copy(texts, both.at[pl.ds(0, rows)], semaphores.at[0]),
        pltpu.make_async_copy(images, both.at[pl.ds(rows, rows)], semaphores.at[1]),
    ]
    for copy in copies:
        copy.start()
    for copy in copies:
        copy.wait()


def join(texts, images):
    rows, width = texts.shape
    return pl.pallas_call(
        join_kernel,
        out_shape=jax.ShapeDtypeStruct((2 * rows, width), BF16),
        in_specs=[pl.BlockSpec(memory_space=pl.ANY)] * 2,
        out_specs=pl.BlockSpec(memory_space=pltpu.VMEM),
        scratch_shapes=[pltpu.SemaphoreType.DMA((2,))],
        compiler_params=pltpu.CompilerParams(vmem_limit_bytes=VMEM_LIMIT),
        cost_estimate=pl.CostEstimate(flops=1000, bytes_accessed=1000, transcendentals=0),
    )(texts, images)


def own_kernel(
    temper, flags, column, row, texts, images, other,
    text_half, image_half, text_other, image_other,
    image_near, image_far, text_near, text_far,
):
    rows = texts.shape[0]
    text, image = half_of(texts[...]), half_of(images[...])
    text_half[...] = text
    image_half[...] = image
    text_other[...] = half_of(other[:rows])
    image_other[...] = half_of(other[rows:])
    target = lax.broadcasted_iota(jnp.int32, (rows, rows), 1)
    image_near[...] = mm(weigh(temper, image, text, column[...] == target), text, NN)
    target = lax.broadcasted_iota(jnp.int32, (rows, rows), 0)
    text_near[...] = mm(weigh(temper, text, image, row[...] == target), image, NN)

    @pl.when(flags[0] == 0)
    def _():
        image_far[...] = mm(weigh(temper, image_other[...], text), text, NN)
        text_far[...] = jnp.zeros(text_far.shape, F32)

    @pl.when(flags[0] == 1)
    def _():
        text_far[...] = mm(weigh(temper, text_other[...], image), image, NN)
        image_far[...] = jnp.zeros(image_far.shape, F32)


def meet(wanted, temper, resident, block, before, after):
    @pl.when(wanted != 0)
    def _():
        after[...] = before[...] + mm(weigh(temper, resident[...], block), block, NN)

    @pl.when(wanted == 0)
    def _():
        after[...] = before[...]


def visit_kernel(
    temper, flags, text, image, image_half, image_other, text_half, text_other,
    image_near_in, image_far_in, text_near_in, text_far_in,
    image_near, image_far, text_near, text_far,
):
    for k, visitor, near_res, far_res, near_in, far_in, near, far in (
        (0, text, image_half, image_other, image_near_in, image_far_in, image_near, image_far),
        (2, image, text_half, text_other, text_near_in, text_far_in, text_near, text_far),
    ):
        block = half_of(visitor[...])
        meet(flags[k], temper, near_res, block, near_in, near)
        meet(flags[k + 1], temper, far_res, block, far_in, far)


def far_kernel(k, temper, flags, visitor, far_res, far_in, half, far):
    block = half_of(visitor[...])
    half[...] = block
    meet(flags[k + 1], temper, far_res, block, far_in, far)


def near_kernel(
    temper, flags, text, image_half, image_in, image, text_half, text_in, image_out, text_out
):
    meet(flags[0], temper, image_half, text[...], image_in, image_out)
    meet(flags[2], temper, text_half, image[...], text_in, text_out)


def finish_kernel(rows, near, received, grad):
    upstream = near[...] + received[...]
    unit, inverse = unit_of(rows[...])
    along = jnp.sum(unit * upstream, axis=-1, keepdims=True)
    grad[...] = inverse * (upstream - unit * along)


STEPS = ({"A": (0, 1), "B": (1, 1), "C": (1, 2), "D": (1, 3)},
         {"A": (0, 1), "B": (0, 2), "C": (1, 2), "D": (1, 3)})
MEETS = ({"A": (1, 1), "B": (0, 1), "C": (1, 1), "D": (1, 0)},
         {"A": (1, 1), "B": (0, 1), "C": (1, 1), "D": (1, 1)})
PLAN = ("DACB", "ADBC")


def plan_of(chip, parity):
    return PLAN[parity]


def hops_of(n_wide, n_narrow):
    chips = n_narrow // 2
    pairs, kinds = [], []
    for k in range(4):
        moves, kind = {}, {}
        for w in range(n_wide):
            for n in range(n_narrow):
                chip, parity = n // 2, n % 2
                plan, steps = plan_of(chip, parity), STEPS[parity]
                before = (0, 0) if k < 2 else steps[plan[k - 2]]
                place = [
                    ((w + a) % n_wide, ((chip + b) % chips) * 2 + parity)
                    for a, b in (before, steps[plan[k]])
                ]
                moves[place[0]] = place[1]
                kind[place[1][1]] = plan[k]
        assert len(moves) == len(set(moves.values())) == n_wide * n_narrow
        pairs.append(moves)
        kinds.append([kind[n] for n in range(n_narrow)])
    return pairs, kinds


def shards(images, texts, labels, log_scale, bias):
    n_wide, n_narrow = lax.axis_size("wide"), lax.axis_size("narrow")
    wide, narrow = lax.axis_index("wide"), lax.axis_index("narrow")
    rows, width = images.shape
    core = narrow % 2
    pairs, kinds = hops_of(n_wide, n_narrow)

    def moved(value, moves):
        flat = [(a * n_narrow + b, c * n_narrow + d) for (a, b), (c, d) in sorted(moves.items())]
        return lax.ppermute(value, AXES, flat)

    def mirrored(moves):
        def turn(place):
            return ((-place[0]) % n_wide, n_narrow - 1 - place[1])

        return {turn(a): turn(b) for a, b in moves.items()}

    def hop(k, text, image):
        return moved(text, pairs[k]), moved(image, mirrored(pairs[k]))

    def swapped(value):
        return moved(
            value,
            {(w, n): (w, n + 1 - 2 * (n % 2)) for w in range(n_wide) for n in range(n_narrow)},
        )

    def flags_of(k):
        table = []
        for n in range(n_narrow):
            m = n_narrow - 1 - n
            line = [*MEETS[n % 2][kinds[k][n]], *MEETS[m % 2][kinds[k][m]]]
            table.append(line)
        return jnp.asarray(table, jnp.int32)[narrow]

    temper = jnp.stack([jnp.exp(log_scale[0]), bias[0]])
    local = labels - (wide * n_narrow + narrow) * rows
    half = jax.ShapeDtypeStruct((rows, width), BF16)
    full = jax.ShapeDtypeStruct((rows, width), F32)

    first = hop(0, texts, images)
    second = hop(1, texts, images)
    other = swapped(join(texts, images))
    flags = core.reshape(1).astype(jnp.int32)
    (text_half, image_half, text_other, image_other, *sums) = call(
        own_kernel,
        [half] * 4 + [full] * 4,
        [temper, flags, local.reshape(rows, 1), local.reshape(1, rows), texts, images, other],
    )
    residents = [image_half, image_other, text_half, text_other]

    def visit(k, visitors, sums):
        return call(
            visit_kernel,
            [full] * 4,
            [temper, flags_of(k), *visitors, *residents, *sums],
            {8: 0, 9: 1, 10: 2, 11: 3},
        )

    *first, a, b, c, d = lax.optimization_barrier((*first, *sums))
    third = hop(2, *first)
    sums = visit(0, first, [a, b, c, d])
    *second, a, b, c, d = lax.optimization_barrier((*second, *sums))
    fourth = hop(3, *second)
    sums = visit(1, second, [a, b, c, d])
    sums = visit(2, third, sums)
    image_near, image_far, text_near, text_far = sums

    def far(k, visitor, other, far_sum):
        kernel = functools.partial(far_kernel, k)
        return call(
            kernel, [half, full], [temper, flags_of(3), visitor, other, far_sum], {4: 1}
        )

    text, image_far = far(0, fourth[0], image_other, image_far)
    image_back = swapped(image_far)
    image, text_far = far(2, fourth[1], text_other, text_far)
    text_back = swapped(text_far)
    image_near, text_near = call(
        near_kernel,
        [full, full],
        [temper, flags_of(3), text, image_half, image_near, image, text_half, text_near],
        {4: 0, 7: 1},
    )
    (grad_images,) = call(finish_kernel, [full], [images, image_near, image_back])
    (grad_texts,) = call(finish_kernel, [full], [texts, text_near, text_back])
    return (grad_images, grad_texts)


def solution(mesh):
    return jax.shard_map(
        shards,
        mesh=mesh,
        in_specs=(P(AXES, None), P(AXES, None), P(AXES), P(), P()),
        out_specs=(P(AXES, None), P(AXES, None)),
        check_vma=False,
    )
```

```python
import functools

import jax
import jax.numpy as jnp
from jax import lax
from jax.experimental import pallas as pl
from jax.experimental.pallas import tpu as pltpu
from jax.sharding import PartitionSpec as P

EPS = 1e-06
AXES = ("wide", "narrow")
NT = (((1,), (1,)), ((), ()))
NN = (((1,), (0,)), ((), ()))
VMEM_LIMIT = 20 * 1024 * 1024
F32 = jnp.float32
BF16 = jnp.bfloat16


def mm(a, b, dims):
    return lax.dot_general(a, b, dims, preferred_element_type=F32)


def unit_of(rows):
    floats = rows.astype(F32)
    inverse = lax.rsqrt(jnp.sum(floats * floats, axis=-1, keepdims=True) + EPS)
    return floats * inverse, inverse


def half_of(rows):
    return unit_of(rows)[0].astype(BF16)


def call(kernel, outs, inputs, aliases=None):
    specs = [
        pl.BlockSpec(memory_space=pltpu.SMEM if x.ndim == 1 else pltpu.VMEM) for x in inputs
    ]
    return pl.pallas_call(
        kernel,
        out_shape=outs,
        in_specs=specs,
        out_specs=[pl.BlockSpec(memory_space=pltpu.VMEM) for _ in outs],
        input_output_aliases=aliases or {},
        compiler_params=pltpu.CompilerParams(vmem_limit_bytes=VMEM_LIMIT),
        cost_estimate=pl.CostEstimate(flops=1000, bytes_accessed=1000, transcendentals=0),
    )(*inputs)


def weigh(temper, resident, block, positive=None):
    scale, offset = temper[0], temper[1]
    residual = jax.nn.sigmoid(scale * mm(resident, block, NT) + offset)
    if positive is not None:
        residual = residual - positive.astype(F32)
    return (scale * residual).astype(BF16)


def own_kernel(
    temper, flags, column, row, texts, images, other,
    text_half, image_half, text_other, image_other,
    image_near, image_far, text_near, text_far,
):
    rows = texts.shape[0]
    text, image = half_of(texts[...]), half_of(images[...])
    text_half[...] = text
    image_half[...] = image
    text_other[...] = half_of(other[:rows])
    image_other[...] = half_of(other[rows:])
    target = lax.broadcasted_iota(jnp.int32, (rows, rows), 1)
    image_near[...] = mm(weigh(temper, image, text, column[...] == target), text, NN)
    target = lax.broadcasted_iota(jnp.int32, (rows, rows), 0)
    text_near[...] = mm(weigh(temper, text, image, row[...] == target), image, NN)

    @pl.when(flags[0] == 0)
    def _():
        image_far[...] = mm(weigh(temper, image_other[...], text), text, NN)
        text_far[...] = jnp.zeros(text_far.shape, F32)

    @pl.when(flags[0] == 1)
    def _():
        text_far[...] = mm(weigh(temper, text_other[...], image), image, NN)
        image_far[...] = jnp.zeros(image_far.shape, F32)


def meet(wanted, temper, resident, block, before, after):
    @pl.when(wanted != 0)
    def _():
        after[...] = before[...] + mm(weigh(temper, resident[...], block), block, NN)

    @pl.when(wanted == 0)
    def _():
        after[...] = before[...]


def visit_kernel(
    temper, flags, text, image, image_half, image_other, text_half, text_other,
    image_near_in, image_far_in, text_near_in, text_far_in,
    image_near, image_far, text_near, text_far,
):
    for k, visitor, near_res, far_res, near_in, far_in, near, far in (
        (0, text, image_half, image_other, image_near_in, image_far_in, image_near, image_far),
        (2, image, text_half, text_other, text_near_in, text_far_in, text_near, text_far),
    ):
        block = half_of(visitor[...])
        meet(flags[k], temper, near_res, block, near_in, near)
        meet(flags[k + 1], temper, far_res, block, far_in, far)


def far_kernel(k, temper, flags, visitor, far_res, far_in, half, far):
    block = half_of(visitor[...])
    half[...] = block
    meet(flags[k + 1], temper, far_res, block, far_in, far)


def near_kernel(k, temper, flags, visitor, near_res, near_in, near):
    meet(flags[k], temper, near_res, visitor[...], near_in, near)


def finish_kernel(rows, near, received, grad, held, semaphores):
    parts = semaphores.shape[0]
    step = rows.shape[0] // parts
    copies = []
    for k in range(parts):
        part = slice(k * step, (k + 1) * step)
        upstream = near[part] + received[part]
        unit, inverse = unit_of(rows[part])
        along = jnp.sum(unit * upstream, axis=-1, keepdims=True)
        held[part] = inverse * (upstream - unit * along)
        copy = pltpu.make_async_copy(held.at[part], grad.at[part], semaphores.at[k])
        copy.start()
        copies.append(copy)
    for copy in copies:
        copy.wait()


def finish(rows, near, received):
    return pl.pallas_call(
        finish_kernel,
        out_shape=jax.ShapeDtypeStruct(near.shape, F32),
        in_specs=[pl.BlockSpec(memory_space=pltpu.VMEM)] * 3,
        out_specs=pl.BlockSpec(memory_space=pl.ANY),
        scratch_shapes=[pltpu.VMEM(near.shape, F32), pltpu.SemaphoreType.DMA((4,))],
        compiler_params=pltpu.CompilerParams(vmem_limit_bytes=VMEM_LIMIT),
        cost_estimate=pl.CostEstimate(flops=1000, bytes_accessed=1000, transcendentals=0),
    )(rows, near, received)


STEPS = ({"A": (0, 1), "B": (1, 1), "C": (1, 2), "D": (1, 3)},
         {"A": (0, 1), "B": (0, 2), "C": (1, 2), "D": (1, 3)})
MEETS = ({"A": (1, 1), "B": (0, 1), "C": (1, 1), "D": (1, 0)},
         {"A": (1, 1), "B": (0, 1), "C": (1, 1), "D": (1, 1)})
PLAN = ("DACB", "ADBC")


def plan_of(chip, parity):
    return PLAN[parity]


def hops_of(n_wide, n_narrow):
    chips = n_narrow // 2
    pairs, kinds = [], []
    for k in range(4):
        moves, kind = {}, {}
        for w in range(n_wide):
            for n in range(n_narrow):
                chip, parity = n // 2, n % 2
                plan, steps = plan_of(chip, parity), STEPS[parity]
                before = (0, 0) if k < 2 else steps[plan[k - 2]]
                place = [
                    ((w + a) % n_wide, ((chip + b) % chips) * 2 + parity)
                    for a, b in (before, steps[plan[k]])
                ]
                moves[place[0]] = place[1]
                kind[place[1][1]] = plan[k]
        assert len(moves) == len(set(moves.values())) == n_wide * n_narrow
        pairs.append(moves)
        kinds.append([kind[n] for n in range(n_narrow)])
    return pairs, kinds


def shards(images, texts, labels, log_scale, bias):
    n_wide, n_narrow = lax.axis_size("wide"), lax.axis_size("narrow")
    wide, narrow = lax.axis_index("wide"), lax.axis_index("narrow")
    rows, width = images.shape
    core = narrow % 2
    pairs, kinds = hops_of(n_wide, n_narrow)

    def moved(value, moves):
        flat = [(a * n_narrow + b, c * n_narrow + d) for (a, b), (c, d) in sorted(moves.items())]
        return lax.ppermute(value, AXES, flat)

    def mirrored(moves):
        def turn(place):
            return ((-place[0]) % n_wide, n_narrow - 1 - place[1])

        return {turn(a): turn(b) for a, b in moves.items()}

    def hop(k, text, image):
        return moved(text, pairs[k]), moved(image, mirrored(pairs[k]))

    def swapped(value):
        return moved(
            value,
            {(w, n): (w, n + 1 - 2 * (n % 2)) for w in range(n_wide) for n in range(n_narrow)},
        )

    def flags_of(k):
        table = []
        for n in range(n_narrow):
            m = n_narrow - 1 - n
            line = [*MEETS[n % 2][kinds[k][n]], *MEETS[m % 2][kinds[k][m]]]
            table.append(line)
        return jnp.asarray(table, jnp.int32)[narrow]

    temper = jnp.stack([jnp.exp(log_scale[0]), bias[0]])
    local = labels - (wide * n_narrow + narrow) * rows
    half = jax.ShapeDtypeStruct((rows, width), BF16)
    full = jax.ShapeDtypeStruct((rows, width), F32)

    first = hop(0, texts, images)
    second = hop(1, texts, images)
    other = swapped(jnp.concatenate([texts, images]))
    flags = core.reshape(1).astype(jnp.int32)
    (text_half, image_half, text_other, image_other, *sums) = call(
        own_kernel,
        [half] * 4 + [full] * 4,
        [temper, flags, local.reshape(rows, 1), local.reshape(1, rows), texts, images, other],
    )
    residents = [image_half, image_other, text_half, text_other]

    def visit(k, visitors, sums):
        return call(
            visit_kernel,
            [full] * 4,
            [temper, flags_of(k), *visitors, *residents, *sums],
            {8: 0, 9: 1, 10: 2, 11: 3},
        )

    *first, a, b, c, d = lax.optimization_barrier((*first, *sums))
    third = hop(2, *first)
    sums = visit(0, first, [a, b, c, d])
    *second, a, b, c, d = lax.optimization_barrier((*second, *sums))
    fourth = hop(3, *second)
    sums = visit(1, second, [a, b, c, d])
    sums = visit(2, third, sums)
    image_near, image_far, text_near, text_far = sums

    def far(k, visitor, other, far_sum):
        kernel = functools.partial(far_kernel, k)
        return call(
            kernel, [half, full], [temper, flags_of(3), visitor, other, far_sum], {4: 1}
        )

    def near(k, visitor, own, near_sum):
        return call(
            functools.partial(near_kernel, k),
            [full],
            [temper, flags_of(3), visitor, own, near_sum],
            {4: 0},
        )[0]

    image, text_far = far(2, fourth[1], text_other, text_far)
    text_back = swapped(text_far)
    text_near = near(2, image, text_half, text_near)
    image_far, text_near = lax.optimization_barrier((image_far, text_near))
    text, image_far = far(0, fourth[0], image_other, image_far)
    image_back = swapped(image_far)
    image_near = near(0, text, image_half, image_near)
    grad_images = finish(images, image_near, image_back)
    grad_texts = finish(texts, text_near, text_back)
    return (grad_images, grad_texts)


def solution(mesh):
    return jax.shard_map(
        shards,
        mesh=mesh,
        in_specs=(P(AXES, None), P(AXES, None), P(AXES), P(), P()),
        out_specs=(P(AXES, None), P(AXES, None)),
        check_vma=False,
    )
```

```python
import functools

import jax
import jax.numpy as jnp
from jax import lax
from jax.experimental import pallas as pl
from jax.experimental.pallas import tpu as pltpu
from jax.sharding import PartitionSpec as P

EPS = 1e-06
AXES = ("wide", "narrow")
NT = (((1,), (1,)), ((), ()))
NN = (((1,), (0,)), ((), ()))
VMEM_LIMIT = 20 * 1024 * 1024
F32 = jnp.float32
BF16 = jnp.bfloat16


def mm(a, b, dims):
    return lax.dot_general(a, b, dims, preferred_element_type=F32)


def unit_of(rows):
    floats = rows.astype(F32)
    inverse = lax.rsqrt(jnp.sum(floats * floats, axis=-1, keepdims=True) + EPS)
    return floats * inverse, inverse


def half_of(rows):
    return unit_of(rows)[0].astype(BF16)


def call(kernel, outs, inputs, aliases=None):
    specs = [
        pl.BlockSpec(memory_space=pltpu.SMEM if x.ndim == 1 else pltpu.VMEM) for x in inputs
    ]
    return pl.pallas_call(
        kernel,
        out_shape=outs,
        in_specs=specs,
        out_specs=[pl.BlockSpec(memory_space=pltpu.VMEM) for _ in outs],
        input_output_aliases=aliases or {},
        compiler_params=pltpu.CompilerParams(vmem_limit_bytes=VMEM_LIMIT),
        cost_estimate=pl.CostEstimate(flops=1000, bytes_accessed=1000, transcendentals=0),
    )(*inputs)


def weigh(temper, resident, block, positive=None):
    scale, offset = temper[0], temper[1]
    residual = jax.nn.sigmoid(scale * mm(resident, block, NT) + offset)
    if positive is not None:
        residual = residual - positive.astype(F32)
    return (scale * residual).astype(BF16)


def own_kernel(
    temper, flags, column, row, texts, images, other,
    text_half, image_half, text_other, image_other,
    image_near, image_far, text_near, text_far,
):
    rows = texts.shape[0]
    text, image = half_of(texts[...]), half_of(images[...])
    text_half[...] = text
    image_half[...] = image
    text_other[...] = half_of(other[:rows])
    image_other[...] = half_of(other[rows:])
    target = lax.broadcasted_iota(jnp.int32, (rows, rows), 1)
    image_near[...] = mm(weigh(temper, image, text, column[...] == target), text, NN)
    target = lax.broadcasted_iota(jnp.int32, (rows, rows), 0)
    text_near[...] = mm(weigh(temper, text, image, row[...] == target), image, NN)

    @pl.when(flags[0] == 0)
    def _():
        image_far[...] = mm(weigh(temper, image_other[...], text), text, NN)
        text_far[...] = jnp.zeros(text_far.shape, F32)

    @pl.when(flags[0] == 1)
    def _():
        text_far[...] = mm(weigh(temper, text_other[...], image), image, NN)
        image_far[...] = jnp.zeros(image_far.shape, F32)


def meet(wanted, temper, resident, block, before, after):
    @pl.when(wanted != 0)
    def _():
        after[...] = before[...] + mm(weigh(temper, resident[...], block), block, NN)

    @pl.when(wanted == 0)
    def _():
        after[...] = before[...]


def visit_kernel(
    temper, flags, text, image, image_half, image_other, text_half, text_other,
    image_near_in, image_far_in, text_near_in, text_far_in,
    image_near, image_far, text_near, text_far,
):
    for k, visitor, near_res, far_res, near_in, far_in, near, far in (
        (0, text, image_half, image_other, image_near_in, image_far_in, image_near, image_far),
        (2, image, text_half, text_other, text_near_in, text_far_in, text_near, text_far),
    ):
        block = half_of(visitor[...])
        meet(flags[k], temper, near_res, block, near_in, near)
        meet(flags[k + 1], temper, far_res, block, far_in, far)


def far_kernel(k, temper, flags, visitor, far_res, far_in, half, far):
    block = half_of(visitor[...])
    half[...] = block
    meet(flags[k + 1], temper, far_res, block, far_in, far)


def near_kernel(k, temper, flags, visitor, near_res, near_in, near):
    meet(flags[k], temper, near_res, visitor[...], near_in, near)


def finish_kernel(rows, near, received, grad, held, semaphores):
    parts = semaphores.shape[0]
    step = rows.shape[0] // parts
    copies = []
    for k in range(parts):
        part = slice(k * step, (k + 1) * step)
        upstream = near[part] + received[part]
        unit, inverse = unit_of(rows[part])
        along = jnp.sum(unit * upstream, axis=-1, keepdims=True)
        held[part] = inverse * (upstream - unit * along)
        copy = pltpu.make_async_copy(held.at[part], grad.at[part], semaphores.at[k])
        copy.start()
        copies.append(copy)
    for copy in copies:
        copy.wait()


def finish(rows, near, received):
    return pl.pallas_call(
        finish_kernel,
        out_shape=jax.ShapeDtypeStruct(near.shape, F32),
        in_specs=[pl.BlockSpec(memory_space=pltpu.VMEM)] * 3,
        out_specs=pl.BlockSpec(memory_space=pl.ANY),
        scratch_shapes=[pltpu.VMEM(near.shape, F32), pltpu.SemaphoreType.DMA((4,))],
        compiler_params=pltpu.CompilerParams(vmem_limit_bytes=VMEM_LIMIT),
        cost_estimate=pl.CostEstimate(flops=1000, bytes_accessed=1000, transcendentals=0),
    )(rows, near, received)


STEPS = ({"A": (0, 1), "B": (1, 1), "C": (1, 2), "D": (1, 3)},
         {"A": (0, 1), "B": (0, 2), "C": (1, 2), "D": (1, 3)})
MEETS = ({"A": (1, 1), "B": (0, 1), "C": (1, 1), "D": (1, 0)},
         {"A": (1, 1), "B": (0, 1), "C": (1, 1), "D": (1, 1)})
PLAN = ("DACB", "ADBC")


def plan_of(chip, parity):
    return PLAN[parity]


def hops_of(n_wide, n_narrow):
    chips = n_narrow // 2
    pairs, kinds = [], []
    for k in range(4):
        moves, kind = {}, {}
        for w in range(n_wide):
            for n in range(n_narrow):
                chip, parity = n // 2, n % 2
                plan, steps = plan_of(chip, parity), STEPS[parity]
                before = (0, 0) if k < 2 else steps[plan[k - 2]]
                place = [
                    ((w + a) % n_wide, ((chip + b) % chips) * 2 + parity)
                    for a, b in (before, steps[plan[k]])
                ]
                moves[place[0]] = place[1]
                kind[place[1][1]] = plan[k]
        assert len(moves) == len(set(moves.values())) == n_wide * n_narrow
        pairs.append(moves)
        kinds.append([kind[n] for n in range(n_narrow)])
    return pairs, kinds


def shards(images, texts, labels, log_scale, bias):
    n_wide, n_narrow = lax.axis_size("wide"), lax.axis_size("narrow")
    wide, narrow = lax.axis_index("wide"), lax.axis_index("narrow")
    rows, width = images.shape
    core = narrow % 2
    pairs, kinds = hops_of(n_wide, n_narrow)

    def moved(value, moves):
        flat = [(a * n_narrow + b, c * n_narrow + d) for (a, b), (c, d) in sorted(moves.items())]
        return lax.ppermute(value, AXES, flat)

    def mirrored(moves):
        def turn(place):
            return ((-place[0]) % n_wide, n_narrow - 1 - place[1])

        return {turn(a): turn(b) for a, b in moves.items()}

    def hop(k, text, image):
        return moved(text, pairs[k]), moved(image, mirrored(pairs[k]))

    def swapped(value):
        return moved(
            value,
            {(w, n): (w, n + 1 - 2 * (n % 2)) for w in range(n_wide) for n in range(n_narrow)},
        )

    def flags_of(k):
        table = []
        for n in range(n_narrow):
            m = n_narrow - 1 - n
            line = [*MEETS[n % 2][kinds[k][n]], *MEETS[m % 2][kinds[k][m]]]
            table.append(line)
        return jnp.asarray(table, jnp.int32)[narrow]

    temper = jnp.stack([jnp.exp(log_scale[0]), bias[0]])
    local = labels - (wide * n_narrow + narrow) * rows
    half = jax.ShapeDtypeStruct((rows, width), BF16)
    full = jax.ShapeDtypeStruct((rows, width), F32)

    first = hop(0, texts, images)
    second = hop(1, texts, images)
    other = swapped(jnp.concatenate([texts, images]))
    flags = core.reshape(1).astype(jnp.int32)
    (text_half, image_half, text_other, image_other, *sums) = call(
        own_kernel,
        [half] * 4 + [full] * 4,
        [temper, flags, local.reshape(rows, 1), local.reshape(1, rows), texts, images, other],
    )
    residents = [image_half, image_other, text_half, text_other]

    def visit(k, visitors, sums):
        return call(
            visit_kernel,
            [full] * 4,
            [temper, flags_of(k), *visitors, *residents, *sums],
            {8: 0, 9: 1, 10: 2, 11: 3},
        )

    first = lax.optimization_barrier(first)
    third = hop(2, *first)
    sums = visit(0, first, sums)
    *second, a, b, c, d = lax.optimization_barrier((*second, *sums))
    fourth = hop(3, *second)
    sums = visit(1, second, [a, b, c, d])
    sums = visit(2, third, sums)
    image_near, image_far, text_near, text_far = sums

    def far(k, visitor, other, far_sum):
        kernel = functools.partial(far_kernel, k)
        return call(
            kernel, [half, full], [temper, flags_of(3), visitor, other, far_sum], {4: 1}
        )

    def near(k, visitor, own, near_sum):
        return call(
            functools.partial(near_kernel, k),
            [full],
            [temper, flags_of(3), visitor, own, near_sum],
            {4: 0},
        )[0]

    image, text_far = far(2, fourth[1], text_other, text_far)
    text_back = swapped(text_far)
    text_near = near(2, image, text_half, text_near)
    image_far, text_near = lax.optimization_barrier((image_far, text_near))
    text, image_far = far(0, fourth[0], image_other, image_far)
    image_back = swapped(image_far)
    image_near = near(0, text, image_half, image_near)
    grad_images = finish(images, image_near, image_back)
    grad_texts = finish(texts, text_near, text_back)
    return (grad_images, grad_texts)


def solution(mesh):
    return jax.shard_map(
        shards,
        mesh=mesh,
        in_specs=(P(AXES, None), P(AXES, None), P(AXES), P(), P()),
        out_specs=(P(AXES, None), P(AXES, None)),
        check_vma=False,
    )
```
